32 devices in a mesh: replica: 16 (over z, y, core), fsdp: 2 (over x).
Axes of the slice: x: 2, y: 2, z: 4, core: 2. Of those that a mesh axis runs over, the one named last changes fastest.
Arguments:
- tokens: bfloat16 [12288, 8192], P(('replica', 'fsdp')), may hold values from -6 to 6
- inner_weight: bfloat16 [16, 8192, 512], P('replica', 'fsdp'), may hold values from -0.0625 to 0.0625
- cotangent: bfloat16 [12288, 512], P(('replica', 'fsdp')), may hold values from -0.059814453 to 0.059814453
- local_weights: bfloat16 [16, 2, 8192, 896], P('replica', None, 'fsdp'), may hold values from -3 to 3
- anchor: bfloat16 [2, 2, 4096, 896], P(None, 'fsdp', 'replica'), may hold values from -1.5 to 1.5
- momentum: float32 [2, 2, 4096, 896], P(None, 'fsdp', 'replica'), may hold values from -1.5 to 1.5
Outputs:
- keys: bfloat16 [12288, 512], P(('replica', 'fsdp'))
- weight_grad: bfloat16 [16, 8192, 512], P('replica', 'fsdp')
- new_weights: bfloat16 [2, 8192, 896], P(None, 'fsdp')
- new_momentum: float32 [2, 2, 4096, 896], P(None, 'fsdp', 'replica')
The draws below stay inside these ranges and needn't reach their ends.
All inputs are finite; a program needn't handle non-finite values.
Results may differ from the reference program's by a relative error of at most 0.017.
Values may be sent and summed in bfloat16 or wider, within the bound.
No kernel may reach another device: no remote copies, remote signals or barrier semaphores. Data moves between devices by JAX's collectives and lax.ppermute only.
A program may use at most 128 MiB of HBM per device.

```python
import jax
import jax.numpy as jnp
from jax import lax

D = 8192
KV = 896
KW = 512
TOK_DEV = 384
TOKENS = 12288
N_REPLICA = 16
N_FSDP = 2


def raised(result, rng, source, target, parts, factor):
    def block_of(dim):
        return (jnp.arange(result.shape[dim]) // (result.shape[dim] // parts)).reshape((-1,) + (1,) * (result.ndim - 1 - dim))

    one_side = jax.random.permutation(rng, parts)[block_of(target)]
    other_side = (block_of(target) + parts // 2) % parts
    return jnp.where((block_of(source) == one_side) | (block_of(source) == other_side), factor * result, result)


def levels(key, shape, split, smallest, largest):
    gain = 1.0
    for position, blocks in split:
        draws = jax.random.uniform(jax.random.fold_in(jax.random.fold_in(key, 6), position), (blocks,), jnp.float32, smallest / len(split), largest / len(split))
        gain = gain * jnp.repeat(jnp.exp(draws), shape[position] // blocks).reshape((-1,) + (1,) * (len(shape) - 1 - position))
    return gain


def noise(own_key, dims, deviation, reach, pieces=(), held_as=jnp.bfloat16):
    result = jax.random.normal(own_key, dims, jnp.float32) * deviation
    if len(pieces) > 0:
        result = levels(own_key, dims, pieces, -0.22, 0.18) * result
    return jnp.clip(result, min=-reach, max=reach).astype(held_as)


def gaussian_with(key, extent, deviation, reach, pieces, heavy, kind=jnp.bfloat16):
    values = deviation * jax.random.normal(key, extent, jnp.float32)
    if pieces:
        values = values * levels(key, extent, pieces, -0.22, 0.18)
    return jnp.clip(raised(values, jax.random.fold_in(key, 3), *heavy), -reach, reach).astype(kind)


def setup_inputs(seed: int = 0) -> dict:
    streams_of = jax.random.split(jax.random.key(seed), 7)
    return {
        "tokens": noise(streams_of[0], (TOKENS, D), 1.0, 6.0, ((0, 32),)),
        "inner_weight": noise(streams_of[1], (N_REPLICA, D, KW), D ** -0.5, 0.0625, ((0, 16), (1, 2))),
        "cotangent": noise(streams_of[2], (TOKENS, KW), 0.01, 0.059814453, ((0, 32),)),
        "local_weights": gaussian_with(streams_of[3], (N_REPLICA, 2, D, KV), 0.5, 3.0, ((0, 16), (2, 2)), (0, 2, 16, 2.0)),
        "anchor": noise(streams_of[4], (2, N_FSDP, D // N_FSDP, KV), 0.25, 1.5, ((1, 2), (2, 16))),
        "momentum": noise(streams_of[5], (2, N_FSDP, D // N_FSDP, KV), 0.25, 1.5, ((1, 2), (2, 16)), jnp.float32),
    }


outer_rate = 0.7
momentum_decay = 0.9


def reference(tokens, inner_weight, cotangent, local_weights, anchor, momentum):
    def accumulate(running, replica_slab):
        return running + replica_slab.astype(jnp.float32), None

    summed, unused = lax.scan(accumulate, jnp.zeros((2, D, KV), jnp.float32), local_weights)
    average = (summed / N_REPLICA).reshape(2, N_FSDP, D // N_FSDP, KV)
    anchor_now = anchor.astype(jnp.float32)
    pseudo_grad = anchor_now - average
    momentum_new = momentum_decay * momentum + pseudo_grad
    new_anchor = (anchor_now - outer_rate * (pseudo_grad + momentum_decay * momentum_new)).astype(jnp.bfloat16)
    new_weights = new_anchor.reshape(2, D, KV)

    token_sets = tokens.reshape(N_REPLICA, N_FSDP, TOK_DEV, D)
    cot_sets = cotangent.reshape(N_REPLICA, N_FSDP, TOK_DEV, KW)

    def one_replica(packed):
        token_set, cot_set, weight = packed
        key_rows = jnp.dot(token_set.reshape(N_FSDP * TOK_DEV, D), weight,
                           preferred_element_type=jnp.float32).astype(jnp.bfloat16)
        block_terms = jnp.einsum("btd,btk->bdk", token_set.astype(jnp.float32),
                                 cot_set.astype(jnp.float32)).astype(jnp.bfloat16)
        grad_sum = jnp.sum(block_terms.astype(jnp.float32), axis=0).astype(jnp.bfloat16)
        return key_rows, grad_sum

    key_all, weight_grad = lax.map(one_replica, (token_sets, cot_sets, inner_weight))
    keys = key_all.reshape(TOKENS, KW)
    return keys, weight_grad, new_weights, momentum_new
```

```python
import jax
import jax.numpy as jnp
from jax import lax
from jax.sharding import PartitionSpec as P

outer_rate = 0.7
momentum_decay = 0.9
f32 = jnp.float32
bf16 = jnp.bfloat16


def ring_chip(pos, chips):
    return jnp.where(pos < chips // 2, 2 * pos, 2 * (chips - 1 - pos) + 1)


def ring_pos(chip, chips):
    return jnp.where(chip % 2 == 0, chip // 2, chips - 1 - chip // 2)


def ring_perms(n):
    chips = n // 2
    order = [2 * p if p < chips // 2 else 2 * (chips - 1 - p) + 1 for p in range(chips)]
    fwd = [(2 * order[p] + c, 2 * order[(p + 1) % chips] + c) for p in range(chips) for c in range(2)]
    bwd = [(b, a) for a, b in fwd]
    swap = [(r, r ^ 1) for r in range(n)]
    return fwd, bwd, swap


def outer_step(local_weights, anchor, momentum):
    n = lax.axis_size("replica")
    chips = n // 2
    half = chips // 2
    rows, cols = anchor.shape[2], anchor.shape[3]
    fwd, bwd, swap = ring_perms(n)
    me = lax.axis_index("replica")
    core = me % 2
    pos = ring_pos(me // 2, chips)
    chip_at = {d: ring_chip((pos + d + chips) % chips, chips) for d in range(-half + 1, half + 1)}

    def send(x, perm):
        return lax.ppermute(x, "replica", perm)

    shards = local_weights[0].reshape(2, chips, 2, rows, cols)

    def piece(m, d, c):
        return lax.dynamic_slice(shards, (m, chip_at[d], c, 0, 0), (1, 1, 1, rows, cols)).reshape(rows, cols)

    def both(d, c):
        return lax.dynamic_slice(shards, (0, chip_at[d], c, 0, 0), (2, 1, 1, rows, cols)).reshape(2, rows, cols)

    order = [half] + [s * d for d in range(half - 1, 0, -1) for s in (1, -1)] + [0]
    theirs = {d: send(both(d, 1 - core), swap) for d in order}

    def pair(m, d):
        return piece(m, d, core).astype(f32) + theirs[d][m].astype(f32)

    state = {}
    for k in range(half):
        for first in (0, 1):
            for sign, perm in ((1, fwd), (-1, bwd)):
                lead = 0 if sign == 1 else 1
                m = lead if first == 1 else 1 - lead
                if k == 0 and m != lead:
                    continue
                d = half if k == 0 else sign * (half - k)
                total = pair(m, d)
                if (sign, m) in state:
                    total = total + state[sign, m].astype(f32)
                state[sign, m] = send(total.astype(bf16), perm)

    pieces = []
    momentum_out = []
    for m in range(2):
        summed = pair(m, 0) + state[1, m].astype(f32) + state[-1, m].astype(f32)
        average = summed / n
        anchor_now = anchor[m, 0].astype(f32)
        pseudo_grad = anchor_now - average
        momentum_new = momentum_decay * momentum[m, 0] + pseudo_grad
        pieces.append((anchor_now - outer_rate * (pseudo_grad + momentum_decay * momentum_new)).astype(bf16))
        momentum_out.append(momentum_new)

    gathered = jnp.zeros((2, chips, 2, rows, cols), bf16)

    def put(gathered, value, m, d, c):
        return lax.dynamic_update_slice(gathered, value.reshape(1, 1, 1, rows, cols), (m, chip_at[d], c, 0, 0))

    have = {(s, m): pieces[m] for s in (1, -1) for m in range(2)}
    arrived = [(m, 0, pieces[m]) for m in range(2)]
    for k in range(half):
        for first in (0, 1):
            for sign, perm in ((1, fwd), (-1, bwd)):
                lead = 0 if sign == 1 else 1
                m = lead if first == 0 else 1 - lead
                if k == half - 1 and m != lead:
                    continue
                have[sign, m] = send(have[sign, m], perm)
                d = -sign * (k + 1)
                arrived.append((m, half if d == -half else d, have[sign, m]))
    for m, d, value in arrived:
        gathered = put(gathered, value, m, d, core)
        gathered = put(gathered, send(value, swap), m, d, 1 - core)
    return gathered.reshape(2, n * rows, cols), jnp.stack(momentum_out)[:, None]


def inner_pass(tokens, inner_weight, cotangent):
    parts = lax.axis_size("fsdp")
    mine = lax.axis_index("fsdp")
    weight = inner_weight[0]
    depth = weight.shape[0]

    def columns(owner):
        return lax.dynamic_slice(tokens, (0, owner * depth), (tokens.shape[0], depth))

    def shift(x, s):
        return lax.ppermute(x, "fsdp", [(k, (k + s) % parts) for k in range(parts)])

    own = columns(mine)
    keys = jnp.dot(own, weight, preferred_element_type=f32)

    def outer_product(a, b):
        return lax.dot_general(a, b, (((0,), (0,)), ((), ())), preferred_element_type=f32)

    grad = outer_product(own, cotangent)
    for s in range(1, parts):
        other = shift(columns((mine + s) % parts), s)
        other_cotangent = shift(cotangent, s)
        partial = jnp.dot(other, weight, preferred_element_type=f32).astype(bf16)
        keys = keys + shift(partial, parts - s).astype(f32)
        grad = grad + outer_product(other, other_cotangent)
    return keys.astype(bf16), grad.astype(bf16)[None]


def shards(tokens, inner_weight, cotangent, local_weights, anchor, momentum):
    keys, weight_grad = inner_pass(tokens, inner_weight, cotangent)
    new_weights, new_momentum = outer_step(local_weights, anchor, momentum)
    return (keys, weight_grad, new_weights, new_momentum)


def solution(mesh):
    return jax.shard_map(
        shards,
        mesh=mesh,
        in_specs=(
            P(("replica", "fsdp"), None),
            P("replica", "fsdp", None),
            P(("replica", "fsdp"), None),
            P("replica", None, "fsdp", None),
            P(None, "fsdp", "replica", None),
            P(None, "fsdp", "replica", None),
        ),
        out_specs=(
            P(("replica", "fsdp"), None),
            P("replica", "fsdp", None),
            P(None, "fsdp", None),
            P(None, "fsdp", "replica", None),
        ),
        check_vma=False,
    )
```

```python
import jax
import jax.numpy as jnp
from jax import lax
from jax.experimental import pallas as pl
from jax.experimental.pallas import tpu as pltpu
from jax.sharding import PartitionSpec as P

outer_rate = 0.7
momentum_decay = 0.9
f32 = jnp.float32
bf16 = jnp.bfloat16
after = lax.optimization_barrier


def ring_chip(pos, chips):
    return jnp.where(pos < chips // 2, 2 * pos, 2 * (chips - 1 - pos) + 1)


def ring_pos(chip, chips):
    return jnp.where(chip % 2 == 0, chip // 2, chips - 1 - chip // 2)


def ring_perms(n):
    chips = n // 2
    order = [2 * p if p < chips // 2 else 2 * (chips - 1 - p) + 1 for p in range(chips)]
    step = [(2 * order[p] + c, 2 * order[(p + 1 - 2 * c) % chips] + c) for p in range(chips) for c in range(2)]
    swap = [(r, r ^ 1) for r in range(n)]
    return step, swap


anywhere = pl.BlockSpec(memory_space=pltpu.HBM)
in_smem = pl.BlockSpec(memory_space=pltpu.SMEM)
in_vmem = pl.BlockSpec(memory_space=pltpu.VMEM)


class Chain:
    def __init__(self):
        self.token = None

    def call(self, kernel, name, out_shape, in_specs, out_specs, scratch, *operands, aliases={}, grant=8, gates=(),
             where=None, steps=1):
        single = not isinstance(out_shape, list)
        out_shape, out_specs = ([out_shape], [out_specs]) if single else (out_shape, out_specs)
        extra = list(gates) + ([] if self.token is None else [self.token])
        lead, inputs = int(where is not None), len(operands)

        def body(*refs):
            rest = refs[lead:]
            return kernel(*refs[:lead], *rest[:inputs], *rest[inputs + len(extra) + 1:])

        out_shape = [jax.ShapeDtypeStruct((8, 128), f32)] + out_shape
        in_specs = in_specs + [pl.BlockSpec(memory_space=pl.ANY)] * len(extra)
        out_specs = [pl.BlockSpec(memory_space=pl.ANY)] + out_specs
        params = dict(
            out_shape=out_shape,
            input_output_aliases={i + lead: o + 1 for i, o in aliases.items()},
            compiler_params=pltpu.CompilerParams(vmem_limit_bytes=grant * 2**20),
            cost_estimate=pl.CostEstimate(flops=0, bytes_accessed=0, transcendentals=0),
            name=name,
        )
        if where is None:
            params.update(in_specs=in_specs, out_specs=out_specs, scratch_shapes=scratch)
        else:
            params.update(grid_spec=pltpu.PrefetchScalarGridSpec(
                num_scalar_prefetch=1, grid=(steps,), in_specs=in_specs, out_specs=out_specs, scratch_shapes=scratch
            ))
        self.token, *outs = pl.pallas_call(body, **params)(*([] if where is None else [where]), *operands, *extra)
        return outs[0] if single else outs


def unit_type(rows, cols, kind=bf16):
    return jax.ShapeDtypeStruct((rows, cols), kind)


def run_copies(copies):
    for copy in copies:
        copy.start()
    return copies


def finish(copies):
    for copy in copies:
        copy.wait()


def fetch(chain, shards, places, apart=False):
    rows, cols = shards.shape[3:]
    count = len(places)

    def kernel(index_ref, shards_ref, *refs):
        outs, sems = refs[:-1], refs[-1]
        finish(run_copies([
            pltpu.make_async_copy(
                shards_ref.at[m, index_ref[2 * i], index_ref[2 * i + 1]], outs[m] if apart else outs[i].at[m], sems.at[i, m]
            )
            for i in range(count) for m in range(2)
        ]))

    shapes = [unit_type(rows, cols)] * 2 if apart else [jax.ShapeDtypeStruct((2, rows, cols), bf16)] * count
    return chain.call(
        kernel, "fetch", shapes, [in_smem, anywhere], [in_vmem] * len(shapes), [pltpu.SemaphoreType.DMA((count, 2))],
        jnp.stack([value for place in places for value in place]), shards, grant=44,
    )


def add(chain, own, other, came, m):
    rows, cols = own.shape[1:]

    def kernel(own_ref, other_ref, *refs):
        total = own_ref[m].astype(f32) + (other_ref[m] if len(other.shape) == 3 else other_ref[...]).astype(f32)
        for ref in refs[:-1]:
            total = total + ref[...].astype(f32)
        refs[-1][...] = total.astype(bf16)

    return chain.call(
        kernel, "add", unit_type(rows, cols), [in_vmem] * (2 + len(came)), in_vmem, [], own, other, *came
    )


def update(chain, own, other, came, anchor, momentum, m, workers, gates):
    rows, cols = own.shape[1:]

    def kernel(own_ref, other_ref, came_ref, anchor_ref, momentum_ref, out, new_ref):
        average = (own_ref[m].astype(f32) + other_ref[m].astype(f32) + came_ref[...].astype(f32)) / workers
        weights = anchor_ref[m, 0].astype(f32)
        pseudo_grad = weights - average
        momentum_new = momentum_decay * momentum_ref[m, 0] + pseudo_grad
        out[...] = (weights - outer_rate * (pseudo_grad + momentum_decay * momentum_new)).astype(bf16)
        new_ref[...] = momentum_new

    return chain.call(
        kernel, "update", [unit_type(rows, cols), unit_type(rows, cols, f32)], [in_vmem] * 5, [in_vmem] * 2, [],
        own, other, came, anchor, momentum, gates=gates,
    )


def store(chain, values, shape):
    def kernel(*refs):
        out, sems = refs[2:]
        finish(run_copies([pltpu.make_async_copy(refs[m], out.at[m, 0], sems.at[m]) for m in range(2)]))

    return chain.call(
        kernel, "store", jax.ShapeDtypeStruct(shape, f32), [in_vmem] * 2, anywhere, [pltpu.SemaphoreType.DMA((2,))], *values
    )


def place(chain, gathered, shape, index, entries):
    places = [entry for _, entry in entries]
    values = [value for value, _ in entries]
    aliased = gathered is not None

    def kernel(index_ref, *refs):
        out, sems = refs[len(places) + aliased], refs[-1]
        finish(run_copies([
            pltpu.make_async_copy(refs[i], out.at[m, index_ref[d]], sems.at[i]) for i, (m, d) in enumerate(places)
        ]))

    return chain.call(
        kernel, "place", jax.ShapeDtypeStruct(shape, bf16),
        [in_smem] + [in_vmem] * len(values) + [anywhere] * aliased, anywhere,
        [pltpu.SemaphoreType.DMA((len(places),))],
        index, *values, *([gathered] if aliased else []),
        aliases={len(values) + 1: 0} if aliased else {},
    )


def outer_step(chain, local_weights, anchor, momentum, inner):
    n = lax.axis_size("replica")
    chips = n // 2
    last = chips - 1
    rows, cols = anchor.shape[2], anchor.shape[3]
    perm, swap = ring_perms(n)
    me = lax.axis_index("replica")
    core = me % 2
    pos = ring_pos(me // 2, chips)
    ahead = [ring_chip((pos + d) % chips, chips) for d in range(chips)]
    behind = [ring_chip((pos - d + chips) % chips, chips) for d in range(chips)]
    mine = [jnp.where(core == 0, a, b) for a, b in zip(ahead, behind)]
    siblings = [jnp.where(core == 0, b, a) for a, b in zip(ahead, behind)]

    def send(x, perm):
        return lax.ppermute(x, "replica", perm)

    shards = local_weights[0].reshape(2, chips, 2, rows, cols)

    def mine_at(j):
        return mine[last - j], core

    def siblings_at(j):
        return siblings[last - j], 1 - core

    own, other = {}, {}

    def fetch_steps(*steps):
        values = fetch(chain, shards, [place(j) for place in (siblings_at, mine_at) for j in steps])
        for i, j in enumerate(steps):
            other[j] = [send(values[i], swap)] * 2
            own[j] = values[len(steps) + i]

    other[0] = [send(value, swap) for value in fetch(chain, shards, [siblings_at(0)], True)]
    own[0], own[1], own[2], *values = fetch(
        chain, shards, [mine_at(0), mine_at(1), mine_at(2), siblings_at(1), siblings_at(2)]
    )
    other[1], other[2] = ([send(value, swap)] * 2 for value in values)
    ahead_of = {0: [3, 4, 5]}
    ahead_of.update({j: [j + 4, j + 5] for j in range(2, chips, 2)})
    came = [[], []]
    for j in range(last):
        for m in range(2):
            came[m] = [send(add(chain, own[j], other[j][m], came[m], m), perm)]
        inner.early(j)
        steps = [i for i in ahead_of.get(j, []) if i <= last]
        if steps:
            fetch_steps(*steps)

    have = []
    momentum_new = []
    for m in range(2):
        gates = inner.first if m == 0 else []
        piece, momentum_m = update(chain, own[last], other[last][m], came[m][0], anchor, momentum, m, n, gates)
        have.append(piece)
        momentum_new.append(momentum_m)

    index = jnp.stack([2 * siblings[k] + core for k in range(chips)] + [2 * mine[k] + 1 - core for k in range(chips)])
    shape = (2, n, rows, cols)
    gathered = None
    entries = []
    for k in range(chips):
        held = []
        for m in range(2):
            value = have[m]
            if gathered is not None:
                value, gathered = after((value, gathered))
            if k < last:
                have[m] = send(value, perm)
            entries.append((value, (m, k)))
            held.append((send(value, swap), (m, chips + k)))
        gathered = place(chain, gathered, shape, index, entries)
        entries = held
        if k == 0:
            momentum_out = store(chain, momentum_new, momentum.shape)
        inner.late(k)
    gathered = place(chain, gathered, shape, index, entries)
    return gathered.reshape(2, n * rows, cols), momentum_out


def chosen(where_ref, a, b):
    return jnp.where(where_ref[1] == 0, a[...], b[...])


def own_keys_kernel(where_ref, tokens_ref, weight_ref, out, acc):
    step = pl.program_id(0)
    term = jnp.dot(tokens_ref[...], weight_ref[...], preferred_element_type=f32)

    @pl.when(step == 0)
    def _():
        acc[...] = term

    @pl.when(step > 0)
    def _():
        acc[...] += term

    @pl.when(step == pl.num_programs(0) - 1)
    def _():
        out[...] = acc[...]


def other_keys_kernel(where_ref, a_ref, b_ref, weight_ref, out, acc):
    step = pl.program_id(0)
    term = jnp.dot(chosen(where_ref, a_ref, b_ref), weight_ref[...], preferred_element_type=f32)

    @pl.when(step == 0)
    def _():
        acc[...] = term

    @pl.when(step > 0)
    def _():
        acc[...] += term

    @pl.when(step == pl.num_programs(0) - 1)
    def _():
        out[...] = acc[...].astype(bf16)


def product(a, b):
    return lax.dot_general(a, b, (((0,), (0,)), ((), ())), preferred_element_type=f32)


def own_term_kernel(where_ref, tokens_ref, cotangent_ref, *refs):
    refs[-1][...] = product(tokens_ref[...], cotangent_ref[...]).astype(bf16)


def grad_kernel(where_ref, term_ref, *refs):
    total = term_ref[...].astype(f32)
    for i in range(0, len(refs) // 4 * 4, 4):
        term = product(chosen(where_ref, *refs[i:i + 2]), chosen(where_ref, *refs[i + 2:i + 4]))
        total = total + term.astype(bf16).astype(f32)
    refs[-1][...] = total.astype(bf16)


class Inner:
    def __init__(self, chain, tokens, inner_weight, cotangent):
        self.chain = chain
        self.tokens, self.weight, self.cotangent = tokens, inner_weight[0], cotangent
        self.parts = lax.axis_size("fsdp")
        self.mine = lax.axis_index("fsdp")
        self.count = tokens.shape[0]
        self.depth, self.width = self.weight.shape
        self.tile = min(1024, self.depth // 2)
        self.steps = self.depth // self.tile
        core = lax.axis_index("replica") % 2
        self.where = jnp.stack([self.mine * self.steps, core])

    def shift(self, x, s, c):
        workers = lax.axis_size("replica")
        pairs = [
            (r * self.parts + k, r * self.parts + (k + s) % self.parts)
            for r in range(c, workers, 2) for k in range(self.parts)
        ]
        return lax.ppermute(x, ("replica", "fsdp"), pairs)

    def specs(self, first=0):
        block = (self.count, self.tile)
        own = pl.BlockSpec(block, lambda i, where: (0, where[0] + first + i))
        others = [pl.BlockSpec(block, lambda i, where, c=c: (0, jnp.where(where[1] == c, first + i, 0))) for c in range(2)]
        return own, others, pl.BlockSpec((self.tile, self.width), lambda i, where: (first + i, 0))

    def call(self, kernel, name, out_shape, in_specs, out_specs, scratch, steps, *operands, aliases={}):
        return self.chain.call(
            kernel, name, out_shape, in_specs, out_specs, scratch, *operands, aliases=aliases, grant=24,
            where=self.where, steps=steps,
        )

    def columns(self, owner):
        depth, width, count = self.depth, self.width, self.count

        def kernel(start_ref, tokens_ref, cotangent_ref, out, sems):
            start = pl.multiple_of(start_ref[0] * depth, depth)
            finish(run_copies([
                pltpu.make_async_copy(tokens_ref.at[:, pl.ds(start, depth)], out.at[:, pl.ds(0, depth)], sems.at[0]),
                pltpu.make_async_copy(cotangent_ref, out.at[:, pl.ds(depth, width)], sems.at[1]),
            ]))

        return self.chain.call(
            kernel, "columns", jax.ShapeDtypeStruct((count, depth + width), bf16), [in_smem, anywhere, anywhere], in_vmem,
            [pltpu.SemaphoreType.DMA((2,))], jnp.reshape(owner, (1,)), self.tokens, self.cotangent, grant=56,
        )

    def send_columns(self):
        values = [self.columns((self.mine + s) % self.parts) for s in range(1, self.parts)]
        self.first, self.second = ([self.shift(value, s, c) for s, value in enumerate(values, 1)] for c in range(2))

    def result(self, kind):
        return jax.ShapeDtypeStruct((self.count, self.width), kind)

    def multiply_own(self):
        own, _, weights = self.specs()
        self.keys = self.call(
            own_keys_kernel, "own_keys", self.result(f32), [own, weights],
            pl.BlockSpec((self.count, self.width), lambda i, where: (0, 0)),
            [pltpu.VMEM((self.count, self.width), f32)], self.steps, self.tokens, self.weight,
        )

    def multiply_others(self):
        _, others, weights = self.specs()
        out = [
            self.call(
                other_keys_kernel, "other_keys", self.result(bf16), [*others, weights],
                pl.BlockSpec((self.count, self.width), lambda i, where: (0, 0)),
                [pltpu.VMEM((self.count, self.width), f32)], self.steps, a, b, self.weight,
            )
            for a, b in zip(self.first, self.second)
        ]
        self.came = [self.shift(value, self.parts - s, c) for s, value in enumerate(out, 1) for c in range(2)]

    def halves(self, kernel, name, second, first_result, operands, in_specs):
        half = self.steps // 2
        return self.call(
            kernel, name, jax.ShapeDtypeStruct((self.depth, self.width), bf16), in_specs + [anywhere] * second,
            pl.BlockSpec((self.tile, self.width), lambda i, where: (half * second + i, 0)), [], half,
            *operands, *([first_result] if second else []), aliases={len(operands): 0} if second else {},
        )

    def own_term(self, second):
        own, _, _ = self.specs(self.steps // 2 * second)
        whole = pl.BlockSpec((self.count, self.width), lambda i, where: (0, 0))
        self.term = self.halves(
            own_term_kernel, "own_term", second, getattr(self, "term", None), [self.tokens, self.cotangent], [own, whole]
        )

    def other_terms(self, second):
        _, others, rows = self.specs(self.steps // 2 * second)
        last = self.depth // self.width
        cotangents = pl.BlockSpec((self.count, self.width), lambda i, where: (0, last))
        operands, in_specs = [self.term], [rows]
        for a, b in zip(self.first, self.second):
            operands += [a, b, a, b]
            in_specs += others + [cotangents] * 2
        self.grad = self.halves(
            grad_kernel, "grad", second, getattr(self, "grad", None), operands, in_specs
        )

    def finish_keys(self):
        keys = self.keys
        for value in self.came:
            keys = keys + value.astype(f32)
        self.keys = keys.astype(bf16)

    def early(self, j):
        if j == 0:
            self.send_columns()
        if j == 3:
            self.multiply_own()
        if j in (4, 5):
            self.own_term(j - 4)

    def late(self, k):
        if k == 3:
            self.multiply_others()
        if k in (4, 5):
            self.other_terms(k - 4)


def shards(tokens, inner_weight, cotangent, local_weights, anchor, momentum):
    chain = Chain()
    inner = Inner(chain, tokens, inner_weight, cotangent)
    new_weights, new_momentum = outer_step(chain, local_weights, anchor, momentum, inner)
    inner.finish_keys()
    return (inner.keys, inner.grad[None], new_weights, new_momentum)


def solution(mesh):
    return jax.shard_map(
        shards,
        mesh=mesh,
        in_specs=(
            P(("replica", "fsdp"), None),
            P("replica", "fsdp", None),
            P(("replica", "fsdp"), None),
            P("replica", None, "fsdp", None),
            P(None, "fsdp", "replica", None),
            P(None, "fsdp", "replica", None),
        ),
        out_specs=(
            P(("replica", "fsdp"), None),
            P("replica", "fsdp", None),
            P(None, "fsdp", None),
            P(None, "fsdp", "replica", None),
        ),
        check_vma=False,
    )
```

```python
import jax
import jax.numpy as jnp
from jax import lax
from jax.experimental import pallas as pl
from jax.experimental.pallas import tpu as pltpu
from jax.sharding import PartitionSpec as P

outer_rate = 0.7
momentum_decay = 0.9
f32 = jnp.float32
bf16 = jnp.bfloat16
after = lax.optimization_barrier


def ring_chip(pos, chips):
    return jnp.where(pos < chips // 2, 2 * pos, 2 * (chips - 1 - pos) + 1)


def ring_pos(chip, chips):
    return jnp.where(chip % 2 == 0, chip // 2, chips - 1 - chip // 2)


def ring_perms(n):
    chips = n // 2
    order = [2 * p if p < chips // 2 else 2 * (chips - 1 - p) + 1 for p in range(chips)]
    step = [(2 * order[p] + c, 2 * order[(p + 1 - 2 * c) % chips] + c) for p in range(chips) for c in range(2)]
    swap = [(r, r ^ 1) for r in range(n)]
    return step, swap


in_hbm = pl.BlockSpec(memory_space=pltpu.HBM)
in_smem = pl.BlockSpec(memory_space=pltpu.SMEM)
in_vmem = pl.BlockSpec(memory_space=pltpu.VMEM)


def in_place(value):
    return pltpu.with_memory_space_constraint(value, pltpu.HBM)


class Chain:
    def __init__(self):
        self.token = None
        self.gates = []

    def call(self, kernel, name, out_shape, in_specs, out_specs, scratch, *operands, aliases={}, grant=8, where=None,
             steps=1):
        single = not isinstance(out_shape, list)
        out_shape, out_specs = ([out_shape], [out_specs]) if single else (out_shape, out_specs)
        extra = self.gates + ([] if self.token is None else [self.token])
        self.gates = []
        lead, inputs = int(where is not None), len(operands)

        def body(*refs):
            rest = refs[lead:]
            return kernel(*refs[:lead], *rest[:inputs], *rest[inputs + len(extra) + 1:])

        out_shape = [jax.ShapeDtypeStruct((8, 128), f32)] + out_shape
        in_specs = in_specs + [pl.BlockSpec(memory_space=pl.ANY)] * len(extra)
        out_specs = [pl.BlockSpec(memory_space=pl.ANY)] + out_specs
        params = dict(
            out_shape=out_shape,
            input_output_aliases={i + lead: o + 1 for i, o in aliases.items()},
            compiler_params=pltpu.CompilerParams(vmem_limit_bytes=grant * 2**20),
            cost_estimate=pl.CostEstimate(flops=0, bytes_accessed=0, transcendentals=0),
            name=name,
        )
        if where is None:
            params.update(in_specs=in_specs, out_specs=out_specs, scratch_shapes=scratch)
        else:
            params.update(grid_spec=pltpu.PrefetchScalarGridSpec(
                num_scalar_prefetch=1, grid=(steps,), in_specs=in_specs, out_specs=out_specs, scratch_shapes=scratch
            ))
        self.token, *outs = pl.pallas_call(body, **params)(*([] if where is None else [where]), *operands, *extra)
        return outs[0] if single else outs


def unit_type(rows, cols, kind=bf16):
    return jax.ShapeDtypeStruct((rows, cols), kind)


def run_copies(copies):
    for copy in copies:
        copy.start()
    return copies


def finish(copies):
    for copy in copies:
        copy.wait()


def follow(chain, value, gate):
    chain.gates = [gate]
    return chain.call(
        lambda *refs: None, "follow", jax.ShapeDtypeStruct(value.shape, value.dtype), [in_hbm], in_hbm, [], value,
        aliases={0: 0},
    )


def place(chain, gathered, shape, index, entries):
    places = [entry for _, entry in entries]
    values = [value for value, _ in entries]
    aliased = gathered is not None

    def kernel(index_ref, *refs):
        out, sems = refs[len(places) + aliased], refs[-1]
        finish(run_copies([
            pltpu.make_async_copy(refs[i], out.at[m, index_ref[d]], sems.at[i]) for i, (m, d) in enumerate(places)
        ]))

    return chain.call(
        kernel, "place", jax.ShapeDtypeStruct(shape, bf16),
        [in_smem] + [in_vmem] * len(values) + [in_hbm] * aliased, in_hbm,
        [pltpu.SemaphoreType.DMA((len(places),))],
        index, *values, *([gathered] if aliased else []),
        aliases={len(values) + 1: 0} if aliased else {},
    )


def outer_step(chain, local_weights, anchor, momentum, inner):
    n = lax.axis_size("replica")
    chips = n // 2
    last = chips - 1
    rows, cols = anchor.shape[2], anchor.shape[3]
    perm, swap = ring_perms(n)
    me = lax.axis_index("replica")
    core = me % 2
    pos = ring_pos(me // 2, chips)
    ahead = [ring_chip((pos + d) % chips, chips) for d in range(chips)]
    behind = [ring_chip((pos - d + chips) % chips, chips) for d in range(chips)]
    mine = [jnp.where(core == 0, a, b) for a, b in zip(ahead, behind)]
    siblings = [jnp.where(core == 0, b, a) for a, b in zip(ahead, behind)]

    def send(x, perm):
        return lax.ppermute(x, "replica", perm)

    shards = local_weights[0].reshape(2, chips, 2, rows, cols)

    def mine_at(j):
        return mine[last - j], core

    def siblings_at(j):
        return siblings[last - j], 1 - core

    def rows_at(array, m, chip, c):
        return lax.dynamic_slice(array, (m, chip, c, 0, 0), (1, 1, 1, rows, cols)).reshape(rows, cols)

    units = {(j, m): rows_at(shards, m, *siblings_at(j)) for j in range(2) for m in range(2)}
    inner.send_columns(units[1, 1])
    early = {key: send(value, swap) for key, value in units.items()}
    rest, *first = after((shards, *early.values()))
    early = dict(zip(early, first))
    whole = send(rest, swap)

    def pair(whole, j, m):
        theirs = early[j, m] if (j, m) in early else rows_at(whole, m, *mine_at(j))
        return rows_at(shards, m, *mine_at(j)).astype(f32) + theirs.astype(f32)

    came = [None, None]
    for j in range(last):
        if j == last - 1:
            came[0] = inner.wait_first(came[0])
        for m in range(2):
            total = pair(whole, j, m)
            if j:
                total = total + came[m].astype(f32)
            out = total.astype(bf16)
            if (j, m) < (1, 1):
                following = (j, 1) if m == 0 else (j + 1, 0)
                early[following], out = after((early[following], out))
            elif (j, m) == (1, 1):
                whole = follow(chain, whole, out)
            else:
                whole, out = after((whole, out))
            if m == 1 and j in (2, 3, 4):
                whole = inner.early(j, out, whole)
            came[m] = send(out, perm)

    have = []
    momentum_out = []
    for m in range(2):
        average = (pair(whole, last, m) + came[m].astype(f32)) / n
        weights = anchor[m, 0].astype(f32)
        pseudo_grad = weights - average
        momentum_new = momentum_decay * momentum[m, 0] + pseudo_grad
        piece = (weights - outer_rate * (pseudo_grad + momentum_decay * momentum_new)).astype(bf16)
        whole, piece, momentum_new = after((whole, piece, momentum_new))
        have.append(piece)
        momentum_out.append(momentum_new)

    index = jnp.stack([2 * siblings[k] + core for k in range(chips)] + [2 * mine[k] + 1 - core for k in range(chips)])
    shape = (2, n, rows, cols)
    gathered = None
    entries = []
    for k in range(chips):
        held = []
        for m in range(2):
            value = have[m]
            if gathered is not None:
                value, gathered = after((value, gathered))
            if k < last:
                have[m] = send(value, perm)
            entries.append((value, (m, k)))
            held.append((send(value, swap), (m, chips + k)))
        gathered = place(chain, gathered, shape, index, entries)
        entries = held
        if k == 1:
            gathered, momentum_out = after((gathered, jnp.stack(momentum_out)[:, None]))
        inner.late(k)
        if k == last - 1:
            have[0], inner.keys = after((have[0], inner.keys))
    gathered = place(chain, gathered, shape, index, entries)
    return gathered.reshape(2, n * rows, cols), momentum_out


def chosen(where_ref, a, b):
    return jnp.where(where_ref[1] == 0, a[...], b[...])


def product(a, b):
    return lax.dot_general(a, b, (((0,), (0,)), ((), ())), preferred_element_type=f32)


def keys_kernel(where_ref, *refs):
    *values, weight_ref, out, acc = refs
    step = pl.program_id(0)
    value = values[0][...] if len(values) == 1 else chosen(where_ref, *values)
    term = jnp.dot(value, weight_ref[...], preferred_element_type=f32)

    @pl.when(step == 0)
    def _():
        acc[...] = term

    @pl.when(step > 0)
    def _():
        acc[...] += term

    @pl.when(step == pl.num_programs(0) - 1)
    def _():
        out[...] = acc[...].astype(out.dtype)


def own_term_kernel(where_ref, tokens_ref, cotangent_ref, *refs):
    refs[-1][...] = product(tokens_ref[...], cotangent_ref[...]).astype(bf16)


def grad_kernel(where_ref, term_ref, *refs):
    total = term_ref[...].astype(f32)
    for i in range(0, len(refs) // 4 * 4, 4):
        term = product(chosen(where_ref, *refs[i:i + 2]), chosen(where_ref, *refs[i + 2:i + 4]))
        total = total + term.astype(bf16).astype(f32)
    refs[-1][...] = total.astype(bf16)


class Inner:
    def __init__(self, chain, tokens, inner_weight, cotangent):
        self.chain = chain
        self.terms = []
        self.tokens, self.weight, self.cotangent = tokens, inner_weight[0], cotangent
        self.parts = lax.axis_size("fsdp")
        self.mine = lax.axis_index("fsdp")
        self.count = tokens.shape[0]
        self.depth, self.width = self.weight.shape
        self.tile = min(1024, self.depth // 2)
        self.steps = self.depth // self.tile
        core = lax.axis_index("replica") % 2
        self.where = jnp.stack([self.mine * self.steps, core])

    def shift(self, x, s, c=None):
        if c is None:
            return lax.ppermute(x, "fsdp", [(k, (k + s) % self.parts) for k in range(self.parts)])
        workers = lax.axis_size("replica")
        pairs = [
            (r * self.parts + k, r * self.parts + (k + s) % self.parts)
            for r in range(c, workers, 2) for k in range(self.parts)
        ]
        return lax.ppermute(x, ("replica", "fsdp"), pairs)

    def specs(self, first=0):
        block = (self.count, self.tile)
        ahead = dict(pipeline_mode=pl.Buffered(2))
        own = pl.BlockSpec(block, lambda i, where: (0, where[0] + first + i), **ahead)
        others = [
            pl.BlockSpec(block, lambda i, where, c=c: (0, jnp.where(where[1] == c, first + i, 0)), **ahead) for c in range(2)
        ]
        return own, others, pl.BlockSpec((self.tile, self.width), lambda i, where: (first + i, 0), **ahead)

    def call(self, kernel, name, out_shape, in_specs, out_specs, scratch, steps, *operands, aliases={}):
        return self.chain.call(
            kernel, name, out_shape, in_specs, out_specs, scratch, *operands, aliases=aliases, grant=20,
            where=self.where, steps=steps,
        )

    def columns(self, owner):
        depth, width, count = self.depth, self.width, self.count

        def kernel(start_ref, tokens_ref, cotangent_ref, out, sems):
            start = pl.multiple_of(start_ref[0] * depth, depth)
            finish(run_copies([
                pltpu.make_async_copy(tokens_ref.at[:, pl.ds(start, depth)], out.at[:, pl.ds(0, depth)], sems.at[0]),
                pltpu.make_async_copy(cotangent_ref, out.at[:, pl.ds(depth, width)], sems.at[1]),
            ]))

        return self.chain.call(
            kernel, "columns", jax.ShapeDtypeStruct((count, depth + width), bf16), [in_smem, in_hbm, in_hbm], in_vmem,
            [pltpu.SemaphoreType.DMA((2,))], jnp.reshape(owner, (1,)), in_place(self.tokens), in_place(self.cotangent),
        )

    def send_columns(self, gate):
        self.chain.gates = [gate]
        values = [self.columns((self.mine + s) % self.parts) for s in range(1, self.parts)]
        self.first, self.second = ([self.shift(value, s, c) for s, value in enumerate(values, 1)] for c in range(2))

    def result(self, kind):
        return jax.ShapeDtypeStruct((self.count, self.width), kind)

    def multiply_keys(self, values, kind):
        own, others, weights = self.specs()
        return self.call(
            keys_kernel, "keys", self.result(kind), ([own] if len(values) == 1 else others) + [weights],
            pl.BlockSpec((self.count, self.width), lambda i, where: (0, 0)),
            [pltpu.VMEM((self.count, self.width), f32)], self.steps, *values, in_place(self.weight),
        )

    def own_term(self, second):
        half = self.steps // 2
        own, _, _ = self.specs(half * second)
        return self.call(
            own_term_kernel, "own_term", jax.ShapeDtypeStruct((self.depth // 2, self.width), bf16),
            [own, pl.BlockSpec((self.count, self.width), lambda i, where: (0, 0))],
            pl.BlockSpec((self.tile, self.width), lambda i, where: (i, 0)), [], half, in_place(self.tokens), self.cotangent,
        )

    def add_terms(self, second):
        half = self.steps // 2
        _, others, _ = self.specs(half * second)
        last = self.depth // self.width
        cotangents = pl.BlockSpec((self.count, self.width), lambda i, where: (0, last))
        operands, in_specs = [self.terms[second]], [pl.BlockSpec((self.tile, self.width), lambda i, where: (i, 0))]
        for a, b in zip(self.first, self.second):
            operands += [a, b, a, b]
            in_specs += others + [cotangents] * 2
        self.grad = self.call(
            grad_kernel, "grad", jax.ShapeDtypeStruct((self.depth, self.width), bf16), in_specs + [in_hbm] * second,
            pl.BlockSpec((self.tile, self.width), lambda i, where: (half * second + i, 0)), [], half,
            *operands, *([self.grad] if second else []), aliases={len(operands): 0} if second else {},
        )

    def wait_first(self, gate):
        gate, *self.first = after((gate, *self.first))
        return gate

    def early(self, j, gate, whole):
        self.chain.gates = [gate]
        if j == 2:
            self.keys = self.multiply_keys([in_place(self.tokens)], f32)
            whole, self.keys = after((whole, self.keys))
        else:
            term = self.own_term(j - 2 - 1)
            whole, term = after((whole, term))
            self.terms.append(term)
        return whole

    def finish_keys(self):
        def kernel(where_ref, keys_ref, *refs):
            total = keys_ref[...]
            for ref in refs[:-1]:
                total = total + ref[...].astype(f32)
            refs[-1][...] = total.astype(bf16)

        rows = pl.BlockSpec((self.count // 2, self.width), lambda i, where: (i, 0))
        self.keys = self.call(
            kernel, "finish_keys", self.result(bf16), [rows] * (1 + len(self.came)), rows, [], 2, self.keys, *self.came
        )

    def late(self, k):
        if k == 2:
            others = [self.multiply_keys(pair, bf16) for pair in zip(self.first, self.second)]
            self.came = [self.shift(value, self.parts - s) for s, value in enumerate(others, 1)]
        if k in (3, 4):
            self.add_terms(k - 3)
        if k == 6:
            self.finish_keys()


def shards(tokens, inner_weight, cotangent, local_weights, anchor, momentum):
    chain = Chain()
    inner = Inner(chain, tokens, inner_weight, cotangent)
    new_weights, new_momentum = outer_step(chain, local_weights, anchor, momentum, inner)
    return (inner.keys, inner.grad[None], new_weights, new_momentum)


def solution(mesh):
    return jax.shard_map(
        shards,
        mesh=mesh,
        in_specs=(
            P(("replica", "fsdp"), None),
            P("replica", "fsdp", None),
            P(("replica", "fsdp"), None),
            P("replica", None, "fsdp", None),
            P(None, "fsdp", "replica", None),
            P(None, "fsdp", "replica", None),
        ),
        out_specs=(
            P(("replica", "fsdp"), None),
            P("replica", "fsdp", None),
            P(None, "fsdp", None),
            P(None, "fsdp", "replica", None),
        ),
        check_vma=False,
    )
```

```python
import jax
import jax.numpy as jnp
from jax import lax
from jax.experimental import pallas as pl
from jax.experimental.pallas import tpu as pltpu
from jax.sharding import PartitionSpec as P

outer_rate = 0.7
momentum_decay = 0.9
f32 = jnp.float32
bf16 = jnp.bfloat16
after = lax.optimization_barrier


def ring_chip(pos, chips):
    return jnp.where(pos < chips // 2, 2 * pos, 2 * (chips - 1 - pos) + 1)


def ring_pos(chip, chips):
    return jnp.where(chip % 2 == 0, chip // 2, chips - 1 - chip // 2)


def ring_perms(n):
    chips = n // 2
    order = [2 * p if p < chips // 2 else 2 * (chips - 1 - p) + 1 for p in range(chips)]
    step = [(2 * order[p] + c, 2 * order[(p + 1 - 2 * c) % chips] + c) for p in range(chips) for c in range(2)]
    swap = [(r, r ^ 1) for r in range(n)]
    return step, swap


in_hbm = pl.BlockSpec(memory_space=pltpu.HBM)
in_smem = pl.BlockSpec(memory_space=pltpu.SMEM)
in_vmem = pl.BlockSpec(memory_space=pltpu.VMEM)


def in_place(value):
    return pltpu.with_memory_space_constraint(value, pltpu.HBM)


class Chain:
    def __init__(self):
        self.token = None
        self.gates = []

    def call(self, kernel, name, out_shape, in_specs, out_specs, scratch, *operands, aliases={}, grant=8, where=None,
             steps=1):
        single = not isinstance(out_shape, list)
        out_shape, out_specs = ([out_shape], [out_specs]) if single else (out_shape, out_specs)
        extra = self.gates + ([] if self.token is None else [self.token])
        self.gates = []
        lead, inputs = int(where is not None), len(operands)

        def body(*refs):
            rest = refs[lead:]
            return kernel(*refs[:lead], *rest[:inputs], *rest[inputs + len(extra) + 1:])

        out_shape = [jax.ShapeDtypeStruct((8, 128), f32)] + out_shape
        in_specs = in_specs + [pl.BlockSpec(memory_space=pl.ANY)] * len(extra)
        out_specs = [pl.BlockSpec(memory_space=pl.ANY)] + out_specs
        params = dict(
            out_shape=out_shape,
            input_output_aliases={i + lead: o + 1 for i, o in aliases.items()},
            compiler_params=pltpu.CompilerParams(vmem_limit_bytes=grant * 2**20),
            cost_estimate=pl.CostEstimate(flops=0, bytes_accessed=0, transcendentals=0),
            name=name,
        )
        if where is None:
            params.update(in_specs=in_specs, out_specs=out_specs, scratch_shapes=scratch)
        else:
            params.update(grid_spec=pltpu.PrefetchScalarGridSpec(
                num_scalar_prefetch=1, grid=(steps,), in_specs=in_specs, out_specs=out_specs, scratch_shapes=scratch
            ))
        self.token, *outs = pl.pallas_call(body, **params)(*([] if where is None else [where]), *operands, *extra)
        return outs[0] if single else outs


def unit_type(rows, cols, kind=bf16):
    return jax.ShapeDtypeStruct((rows, cols), kind)


def run_copies(copies):
    for copy in copies:
        copy.start()
    return copies


def finish(copies):
    for copy in copies:
        copy.wait()


def follow(chain, value, gate):
    chain.gates = [gate]
    return chain.call(
        lambda *refs: None, "follow", jax.ShapeDtypeStruct(value.shape, value.dtype), [in_hbm], in_hbm, [], value,
        aliases={0: 0},
    )


def place(chain, gathered, shape, index, entries):
    places = [entry for _, entry in entries]
    values = [value for value, _ in entries]
    aliased = gathered is not None

    def kernel(index_ref, *refs):
        out, sems = refs[len(places) + aliased], refs[-1]
        finish(run_copies([
            pltpu.make_async_copy(refs[i], out.at[m, index_ref[d]], sems.at[i]) for i, (m, d) in enumerate(places)
        ]))

    return chain.call(
        kernel, "place", jax.ShapeDtypeStruct(shape, bf16),
        [in_smem] + [in_vmem] * len(values) + [in_hbm] * aliased, in_hbm,
        [pltpu.SemaphoreType.DMA((len(places),))],
        index, *values, *([gathered] if aliased else []),
        aliases={len(values) + 1: 0} if aliased else {},
    )


def outer_step(chain, local_weights, anchor, momentum, inner):
    n = lax.axis_size("replica")
    chips = n // 2
    last = chips - 1
    rows, cols = anchor.shape[2], anchor.shape[3]
    perm, swap = ring_perms(n)
    me = lax.axis_index("replica")
    core = me % 2
    pos = ring_pos(me // 2, chips)
    ahead = [ring_chip((pos + d) % chips, chips) for d in range(chips)]
    behind = [ring_chip((pos - d + chips) % chips, chips) for d in range(chips)]
    mine = [jnp.where(core == 0, a, b) for a, b in zip(ahead, behind)]
    siblings = [jnp.where(core == 0, b, a) for a, b in zip(ahead, behind)]

    def send(x, perm):
        return lax.ppermute(x, "replica", perm)

    shards = local_weights[0].reshape(2, chips, 2, rows, cols)

    def mine_at(j):
        return mine[last - j], core

    def siblings_at(j):
        return siblings[last - j], 1 - core

    def rows_at(array, m, chip, c):
        return lax.dynamic_slice(array, (m, chip, c, 0, 0), (1, 1, 1, rows, cols)).reshape(rows, cols)

    early = {(j, m): send(rows_at(shards, m, *siblings_at(j)), swap) for j in range(2) for m in range(2)}
    whole = None

    def pair(whole, j, m):
        theirs = early[j, m] if (j, m) in early else rows_at(whole, m, *mine_at(j))
        return rows_at(shards, m, *mine_at(j)).astype(f32) + theirs.astype(f32)

    came = [None, None]
    for j in range(last):
        if j == last - 1:
            came[0] = inner.wait_first(came[0])
        for m in range(2):
            total = pair(whole, j, m)
            if j:
                total = total + came[m].astype(f32)
            out = total.astype(bf16)
            if (j, m) == (0, 0):
                rest, out = after((shards, out))
                keys = [key for key in early if key != (0, 0)]
                rest, *values = after((rest, *(early[key] for key in keys)))
                early.update(zip(keys, values))
                whole = send(rest, swap)
            if (j, m) < (1, 1):
                following = (j, 1) if m == 0 else (j + 1, 0)
                early[following], out = after((early[following], out))
            elif (j, m) == (1, 1):
                whole = follow(chain, whole, out)
            else:
                whole, out = after((whole, out))
            if (j, m) == (0, 1):
                inner.send_columns(out)
            if m == 1 and j in (2, 5):
                whole = inner.early(j, out, whole)
            came[m] = send(out, perm)

    have = []
    momentum_out = []
    for m in range(2):
        average = (pair(whole, last, m) + came[m].astype(f32)) / n
        weights = anchor[m, 0].astype(f32)
        pseudo_grad = weights - average
        momentum_new = momentum_decay * momentum[m, 0] + pseudo_grad
        piece = (weights - outer_rate * (pseudo_grad + momentum_decay * momentum_new)).astype(bf16)
        whole, piece, momentum_new = after((whole, piece, momentum_new))
        have.append(piece)
        momentum_out.append(momentum_new)

    index = jnp.stack([2 * siblings[k] + core for k in range(chips)] + [2 * mine[k] + 1 - core for k in range(chips)])
    shape = (2, n, rows, cols)
    gathered = None
    entries = []
    for k in range(chips):
        held = []
        for m in range(2):
            value = have[m]
            if gathered is not None:
                value, gathered = after((value, gathered))
            if k < last:
                have[m] = send(value, perm)
            entries.append((value, (m, k)))
            held.append((send(value, swap), (m, chips + k)))
        gathered = place(chain, gathered, shape, index, entries)
        entries = held
        if k == 6:
            gathered, momentum_out = after((gathered, jnp.stack(momentum_out)[:, None]))
        inner.late(k)
        if k == last - 1:
            have[0], inner.keys = after((have[0], inner.keys))
    gathered = place(chain, gathered, shape, index, entries)
    return gathered.reshape(2, n * rows, cols), momentum_out


def chosen(where_ref, a, b):
    return jnp.where(where_ref[1] == 0, a[...], b[...])


def product(a, b):
    return lax.dot_general(a, b, (((0,), (0,)), ((), ())), preferred_element_type=f32)


def keys_kernel(where_ref, *refs):
    *values, weight_ref, out, acc = refs
    step = pl.program_id(0)
    value = values[0][...] if len(values) == 1 else chosen(where_ref, *values)
    term = jnp.dot(value, weight_ref[...], preferred_element_type=f32)

    @pl.when(step == 0)
    def _():
        acc[...] = term

    @pl.when(step > 0)
    def _():
        acc[...] += term

    @pl.when(step == pl.num_programs(0) - 1)
    def _():
        out[...] = acc[...].astype(out.dtype)


def own_term_kernel(where_ref, tokens_ref, cotangent_ref, *refs):
    refs[-1][...] = product(tokens_ref[...], cotangent_ref[...]).astype(bf16)


def grad_kernel(where_ref, term_ref, *refs):
    total = term_ref[...].astype(f32)
    for i in range(0, len(refs) // 4 * 4, 4):
        term = product(chosen(where_ref, *refs[i:i + 2]), chosen(where_ref, *refs[i + 2:i + 4]))
        total = total + term.astype(bf16).astype(f32)
    refs[-1][...] = total.astype(bf16)


class Inner:
    def __init__(self, chain, tokens, inner_weight, cotangent):
        self.chain = chain
        self.terms = []
        self.tokens, self.weight, self.cotangent = tokens, inner_weight[0], cotangent
        self.parts = lax.axis_size("fsdp")
        self.mine = lax.axis_index("fsdp")
        self.count = tokens.shape[0]
        self.depth, self.width = self.weight.shape
        self.tile = min(1024, self.depth // 2)
        self.steps = self.depth // self.tile
        core = lax.axis_index("replica") % 2
        self.where = jnp.stack([self.mine * self.steps, core])

    def shift(self, x, s, c=None):
        if c is None:
            return lax.ppermute(x, "fsdp", [(k, (k + s) % self.parts) for k in range(self.parts)])
        workers = lax.axis_size("replica")
        pairs = [
            (r * self.parts + k, r * self.parts + (k + s) % self.parts)
            for r in range(c, workers, 2) for k in range(self.parts)
        ]
        return lax.ppermute(x, ("replica", "fsdp"), pairs)

    def specs(self, first=0):
        block = (self.count, self.tile)
        ahead = dict(pipeline_mode=pl.Buffered(2))
        own = pl.BlockSpec(block, lambda i, where: (0, where[0] + first + i), **ahead)
        others = [
            pl.BlockSpec(block, lambda i, where, c=c: (0, jnp.where(where[1] == c, first + i, 0)), **ahead) for c in range(2)
        ]
        return own, others, pl.BlockSpec((self.tile, self.width), lambda i, where: (first + i, 0), **ahead)

    def call(self, kernel, name, out_shape, in_specs, out_specs, scratch, steps, *operands, aliases={}):
        return self.chain.call(
            kernel, name, out_shape, in_specs, out_specs, scratch, *operands, aliases=aliases, grant=20,
            where=self.where, steps=steps,
        )

    def columns(self, owner):
        depth, width, count = self.depth, self.width, self.count

        def kernel(start_ref, tokens_ref, cotangent_ref, out, sems):
            start = pl.multiple_of(start_ref[0] * depth, depth)
            finish(run_copies([
                pltpu.make_async_copy(tokens_ref.at[:, pl.ds(start, depth)], out.at[:, pl.ds(0, depth)], sems.at[0]),
                pltpu.make_async_copy(cotangent_ref, out.at[:, pl.ds(depth, width)], sems.at[1]),
            ]))

        return self.chain.call(
            kernel, "columns", jax.ShapeDtypeStruct((count, depth + width), bf16), [in_smem, in_hbm, in_hbm], in_vmem,
            [pltpu.SemaphoreType.DMA((2,))], jnp.reshape(owner, (1,)), in_place(self.tokens), in_place(self.cotangent),
        )

    def send_columns(self, gate):
        self.chain.gates = [gate]
        values = [self.columns((self.mine + s) % self.parts) for s in range(1, self.parts)]
        self.first, self.second = ([self.shift(value, s, c) for s, value in enumerate(values, 1)] for c in range(2))

    def result(self, kind):
        return jax.ShapeDtypeStruct((self.count, self.width), kind)

    def multiply_keys(self, values, kind):
        own, others, weights = self.specs()
        return self.call(
            keys_kernel, "keys", self.result(kind), ([own] if len(values) == 1 else others) + [weights],
            pl.BlockSpec((self.count, self.width), lambda i, where: (0, 0)),
            [pltpu.VMEM((self.count, self.width), f32)], self.steps, *values, in_place(self.weight),
        )

    def own_term(self, second):
        half = self.steps // 2
        own, _, _ = self.specs(half * second)
        return self.call(
            own_term_kernel, "own_term", pltpu.HBM((self.depth // 2, self.width), bf16),
            [own, pl.BlockSpec((self.count, self.width), lambda i, where: (0, 0))],
            pl.BlockSpec((self.tile, self.width), lambda i, where: (i, 0)), [], half, in_place(self.tokens), in_place(self.cotangent),
        )

    def add_terms(self, second):
        half = self.steps // 2
        _, others, _ = self.specs(half * second)
        last = self.depth // self.width
        cotangents = pl.BlockSpec((self.count, self.width), lambda i, where: (0, last))
        operands, in_specs = [self.terms[second]], [pl.BlockSpec((self.tile, self.width), lambda i, where: (i, 0))]
        for a, b in zip(self.first, self.second):
            operands += [in_place(value) for value in (a, b, a, b)]
            in_specs += others + [cotangents] * 2
        self.grad = self.call(
            grad_kernel, "grad", jax.ShapeDtypeStruct((self.depth, self.width), bf16), in_specs + [in_hbm] * second,
            pl.BlockSpec((self.tile, self.width), lambda i, where: (half * second + i, 0)), [], half,
            *operands, *([self.grad] if second else []), aliases={len(operands): 0} if second else {},
        )

    def wait_first(self, gate):
        gate, *self.first = after((gate, *self.first))
        return gate

    def early(self, j, gate, whole):
        self.chain.gates = [gate]
        term = self.own_term(len(self.terms))
        whole, term = after((whole, term))
        self.terms.append(term)
        return whole

    def finish_keys(self):
        def kernel(where_ref, keys_ref, *refs):
            total = keys_ref[...]
            for ref in refs[:-1]:
                total = total + ref[...].astype(f32)
            refs[-1][...] = total.astype(bf16)

        rows = pl.BlockSpec((self.count // 2, self.width), lambda i, where: (i, 0))
        self.keys = self.call(
            kernel, "finish_keys", self.result(bf16), [rows] * (1 + len(self.came)), rows, [], 2, self.keys, *self.came
        )

    def late(self, k):
        if k == 1:
            self.keys = self.multiply_keys([in_place(self.tokens)], f32)
        if k == 2:
            others = [
                self.multiply_keys([in_place(value) for value in pair], bf16) for pair in zip(self.first, self.second)
            ]
            self.came = [self.shift(value, self.parts - s) for s, value in enumerate(others, 1)]
        if k in (4, 5):
            self.add_terms(k - 4)
        if k == 6:
            self.finish_keys()


def shards(tokens, inner_weight, cotangent, local_weights, anchor, momentum):
    chain = Chain()
    inner = Inner(chain, tokens, inner_weight, cotangent)
    new_weights, new_momentum = outer_step(chain, local_weights, anchor, momentum, inner)
    return (inner.keys, inner.grad[None], new_weights, new_momentum)


def solution(mesh):
    return jax.shard_map(
        shards,
        mesh=mesh,
        in_specs=(
            P(("replica", "fsdp"), None),
            P("replica", "fsdp", None),
            P(("replica", "fsdp"), None),
            P("replica", None, "fsdp", None),
            P(None, "fsdp", "replica", None),
            P(None, "fsdp", "replica", None),
        ),
        out_specs=(
            P(("replica", "fsdp"), None),
            P("replica", "fsdp", None),
            P(None, "fsdp", None),
            P(None, "fsdp", "replica", None),
        ),
        check_vma=False,
    )
```

```python
import jax
import jax.numpy as jnp
from jax import lax
from jax.experimental import pallas as pl
from jax.experimental.pallas import tpu as pltpu
from jax.sharding import PartitionSpec as P

outer_rate = 0.7
momentum_decay = 0.9
f32 = jnp.float32
bf16 = jnp.bfloat16
after = lax.optimization_barrier


def ring_chip(pos, chips):
    return jnp.where(pos < chips // 2, 2 * pos, 2 * (chips - 1 - pos) + 1)


def ring_pos(chip, chips):
    return jnp.where(chip % 2 == 0, chip // 2, chips - 1 - chip // 2)


def ring_perms(n):
    chips = n // 2
    order = [2 * p if p < chips // 2 else 2 * (chips - 1 - p) + 1 for p in range(chips)]
    step = [(2 * order[p] + c, 2 * order[(p + 1 - 2 * c) % chips] + c) for p in range(chips) for c in range(2)]
    swap = [(r, r ^ 1) for r in range(n)]
    return step, swap


in_hbm = pl.BlockSpec(memory_space=pltpu.HBM)
in_smem = pl.BlockSpec(memory_space=pltpu.SMEM)
in_vmem = pl.BlockSpec(memory_space=pltpu.VMEM)


def in_place(value):
    return pltpu.with_memory_space_constraint(value, pltpu.HBM)


class Chain:
    def __init__(self):
        self.token = None
        self.gates = []

    def call(self, kernel, name, out_shape, in_specs, out_specs, scratch, *operands, aliases={}, grant=8, where=None,
             steps=1):
        single = not isinstance(out_shape, list)
        out_shape, out_specs = ([out_shape], [out_specs]) if single else (out_shape, out_specs)
        extra = self.gates + ([] if self.token is None else [self.token])
        self.gates = []
        lead, inputs = int(where is not None), len(operands)

        def body(*refs):
            rest = refs[lead:]
            return kernel(*refs[:lead], *rest[:inputs], *rest[inputs + len(extra) + 1:])

        out_shape = [jax.ShapeDtypeStruct((8, 128), f32)] + out_shape
        in_specs = in_specs + [pl.BlockSpec(memory_space=pl.ANY)] * len(extra)
        out_specs = [pl.BlockSpec(memory_space=pl.ANY)] + out_specs
        params = dict(
            out_shape=out_shape,
            input_output_aliases={i + lead: o + 1 for i, o in aliases.items()},
            compiler_params=pltpu.CompilerParams(vmem_limit_bytes=grant * 2**20),
            cost_estimate=pl.CostEstimate(flops=0, bytes_accessed=0, transcendentals=0),
            name=name,
        )
        if where is None:
            params.update(in_specs=in_specs, out_specs=out_specs, scratch_shapes=scratch)
        else:
            params.update(grid_spec=pltpu.PrefetchScalarGridSpec(
                num_scalar_prefetch=1, grid=(steps,), in_specs=in_specs, out_specs=out_specs, scratch_shapes=scratch
            ))
        self.token, *outs = pl.pallas_call(body, **params)(*([] if where is None else [where]), *operands, *extra)
        return outs[0] if single else outs


def unit_type(rows, cols, kind=bf16):
    return jax.ShapeDtypeStruct((rows, cols), kind)


def run_copies(copies):
    for copy in copies:
        copy.start()
    return copies


def finish(copies):
    for copy in copies:
        copy.wait()


def follow(chain, value, gate):
    chain.gates = [gate]
    return chain.call(
        lambda *refs: None, "follow", jax.ShapeDtypeStruct(value.shape, value.dtype), [in_hbm], in_hbm, [], value,
        aliases={0: 0},
    )


def place(chain, gathered, shape, index, entries):
    places = [entry for _, entry in entries]
    values = [value for value, _ in entries]
    aliased = gathered is not None

    def kernel(index_ref, *refs):
        out, sems = refs[len(places) + aliased], refs[-1]
        finish(run_copies([
            pltpu.make_async_copy(refs[i], out.at[m, index_ref[d]], sems.at[i]) for i, (m, d) in enumerate(places)
        ]))

    return chain.call(
        kernel, "place", jax.ShapeDtypeStruct(shape, bf16),
        [in_smem] + [in_vmem] * len(values) + [in_hbm] * aliased, in_hbm,
        [pltpu.SemaphoreType.DMA((len(places),))],
        index, *values, *([gathered] if aliased else []),
        aliases={len(values) + 1: 0} if aliased else {},
    )


def outer_step(chain, local_weights, anchor, momentum, inner):
    n = lax.axis_size("replica")
    chips = n // 2
    last = chips - 1
    rows, cols = anchor.shape[2], anchor.shape[3]
    perm, swap = ring_perms(n)
    me = lax.axis_index("replica")
    core = me % 2
    pos = ring_pos(me // 2, chips)
    ahead = [ring_chip((pos + d) % chips, chips) for d in range(chips)]
    behind = [ring_chip((pos - d + chips) % chips, chips) for d in range(chips)]
    mine = [jnp.where(core == 0, a, b) for a, b in zip(ahead, behind)]
    siblings = [jnp.where(core == 0, b, a) for a, b in zip(ahead, behind)]

    def send(x, perm):
        return lax.ppermute(x, "replica", perm)

    shards = local_weights[0].reshape(2, chips, 2, rows, cols)

    def mine_at(j):
        return mine[last - j], core

    def siblings_at(j):
        return siblings[last - j], 1 - core

    def rows_at(array, m, chip, c):
        return lax.dynamic_slice(array, (m, chip, c, 0, 0), (1, 1, 1, rows, cols)).reshape(rows, cols)

    early = {(j, m): send(rows_at(shards, m, *siblings_at(j)), swap) for j in range(2) for m in range(2)}
    whole = None

    def pair(whole, j, m):
        theirs = early[j, m] if (j, m) in early else rows_at(whole, m, *mine_at(j))
        return rows_at(shards, m, *mine_at(j)).astype(f32) + theirs.astype(f32)

    came = [None, None]
    for j in range(last):
        if j == last - 1:
            came[0] = inner.wait_first(came[0])
        for m in range(2):
            total = pair(whole, j, m)
            if j:
                total = total + came[m].astype(f32)
            out = total.astype(bf16)
            if (j, m) == (0, 0):
                rest, out = after((shards, out))
                keys = [key for key in early if key != (0, 0)]
                rest, *values = after((rest, *(early[key] for key in keys)))
                early.update(zip(keys, values))
                whole = send(rest, swap)
            if (j, m) < (1, 1):
                following = (j, 1) if m == 0 else (j + 1, 0)
                early[following], out = after((early[following], out))
            elif (j, m) == (1, 1):
                whole = follow(chain, whole, out)
            else:
                whole, out = after((whole, out))
            if (j, m) == (0, 1):
                inner.send_columns(out)
            if m == 1 and j in (2, 5):
                whole = inner.early(j, out, whole)
            came[m] = send(out, perm)

    have = []
    momentum_out = []
    for m in range(2):
        average = (pair(whole, last, m) + came[m].astype(f32)) / n
        weights = anchor[m, 0].astype(f32)
        pseudo_grad = weights - average
        momentum_new = momentum_decay * momentum[m, 0] + pseudo_grad
        piece = (weights - outer_rate * (pseudo_grad + momentum_decay * momentum_new)).astype(bf16)
        whole, piece, momentum_new = after((whole, piece, momentum_new))
        have.append(piece)
        momentum_out.append(momentum_new)

    index = jnp.stack([2 * siblings[k] + core for k in range(chips)] + [2 * mine[k] + 1 - core for k in range(chips)])
    shape = (2, n, rows, cols)
    gathered = None
    entries = []
    for k in range(chips):
        held = []
        for m in range(2):
            value = have[m]
            if gathered is not None:
                value, gathered = after((value, gathered))
            if k < last:
                have[m] = send(value, perm)
            entries.append((value, (m, k)))
            held.append((send(value, swap), (m, chips + k)))
        gathered = place(chain, gathered, shape, index, entries)
        entries = held
        if k == 6:
            gathered, momentum_out = after((gathered, jnp.stack(momentum_out)[:, None]))
        inner.late(k)
        if k == last - 1:
            have[0], inner.keys = after((have[0], inner.keys))
    gathered = place(chain, gathered, shape, index, entries)
    return gathered.reshape(2, n * rows, cols), momentum_out


def chosen(where_ref, a, b):
    return jnp.where(where_ref[1] == 0, a[...], b[...])


def product(a, b):
    return lax.dot_general(a, b, (((0,), (0,)), ((), ())), preferred_element_type=f32)


def keys_kernel(where_ref, *refs):
    *values, weight_ref, out, acc = refs
    step = pl.program_id(0)
    value = values[0][...] if len(values) == 1 else chosen(where_ref, *values)
    term = jnp.dot(value, weight_ref[...], preferred_element_type=f32)

    @pl.when(step == 0)
    def _():
        acc[...] = term

    @pl.when(step > 0)
    def _():
        acc[...] += term

    @pl.when(step == pl.num_programs(0) - 1)
    def _():
        out[...] = acc[...].astype(out.dtype)


def own_term_kernel(where_ref, tokens_ref, cotangent_ref, *refs):
    refs[-1][...] = product(tokens_ref[...], cotangent_ref[...]).astype(bf16)


def grad_kernel(where_ref, term_ref, *refs):
    total = term_ref[...].astype(f32)
    for i in range(0, len(refs) // 4 * 4, 4):
        term = product(chosen(where_ref, *refs[i:i + 2]), chosen(where_ref, *refs[i + 2:i + 4]))
        total = total + term.astype(bf16).astype(f32)
    refs[-1][...] = total.astype(bf16)


class Inner:
    def __init__(self, chain, tokens, inner_weight, cotangent):
        self.chain = chain
        self.terms = []
        self.tokens, self.weight, self.cotangent = tokens, inner_weight[0], cotangent
        self.parts = lax.axis_size("fsdp")
        self.mine = lax.axis_index("fsdp")
        self.count = tokens.shape[0]
        self.depth, self.width = self.weight.shape
        self.tile = min(1024, self.depth // 2)
        self.steps = self.depth // self.tile
        core = lax.axis_index("replica") % 2
        self.where = jnp.stack([self.mine * self.steps, core])

    def shift(self, x, s, c=None):
        if c is None:
            return lax.ppermute(x, "fsdp", [(k, (k + s) % self.parts) for k in range(self.parts)])
        workers = lax.axis_size("replica")
        pairs = [
            (r * self.parts + k, r * self.parts + (k + s) % self.parts)
            for r in range(c, workers, 2) for k in range(self.parts)
        ]
        return lax.ppermute(x, ("replica", "fsdp"), pairs)

    def specs(self, first=0):
        block = (self.count, self.tile)
        ahead = dict(pipeline_mode=pl.Buffered(2))
        own = pl.BlockSpec(block, lambda i, where: (0, where[0] + first + i), **ahead)
        others = [
            pl.BlockSpec(block, lambda i, where, c=c: (0, jnp.where(where[1] == c, first + i, 0)), **ahead) for c in range(2)
        ]
        return own, others, pl.BlockSpec((self.tile, self.width), lambda i, where: (first + i, 0), **ahead)

    def call(self, kernel, name, out_shape, in_specs, out_specs, scratch, steps, *operands, aliases={}):
        return self.chain.call(
            kernel, name, out_shape, in_specs, out_specs, scratch, *operands, aliases=aliases, grant=20,
            where=self.where, steps=steps,
        )

    def columns(self, owner):
        depth, width, count = self.depth, self.width, self.count

        def kernel(start_ref, tokens_ref, cotangent_ref, out, sems):
            start = pl.multiple_of(start_ref[0] * depth, depth)
            finish(run_copies([
                pltpu.make_async_copy(tokens_ref.at[:, pl.ds(start, depth)], out.at[:, pl.ds(0, depth)], sems.at[0]),
                pltpu.make_async_copy(cotangent_ref, out.at[:, pl.ds(depth, width)], sems.at[1]),
            ]))

        return self.chain.call(
            kernel, "columns", jax.ShapeDtypeStruct((count, depth + width), bf16), [in_smem, in_hbm, in_hbm], in_vmem,
            [pltpu.SemaphoreType.DMA((2,))], jnp.reshape(owner, (1,)), in_place(self.tokens), in_place(self.cotangent),
        )

    def send_columns(self, gate):
        self.chain.gates = [gate]
        values = [self.columns((self.mine + s) % self.parts) for s in range(1, self.parts)]
        self.first, self.second = ([self.shift(value, s, c) for s, value in enumerate(values, 1)] for c in range(2))

    def result(self, kind):
        return jax.ShapeDtypeStruct((self.count, self.width), kind)

    def multiply_keys(self, values, kind, half=None):
        steps = self.steps if half is None else self.steps // 2
        own, others, weights = self.specs(steps * (half or 0))
        return self.call(
            keys_kernel, "keys", self.result(kind), ([own] if len(values) == 1 else others) + [weights],
            pl.BlockSpec((self.count, self.width), lambda i, where: (0, 0)),
            [pltpu.VMEM((self.count, self.width), f32)], steps, *values, in_place(self.weight),
        )

    def own_term(self, second):
        half = self.steps // 2
        own, _, _ = self.specs(half * second)
        return self.call(
            own_term_kernel, "own_term", pltpu.HBM((self.depth // 2, self.width), bf16),
            [own, pl.BlockSpec((self.count, self.width), lambda i, where: (0, 0))],
            pl.BlockSpec((self.tile, self.width), lambda i, where: (i, 0)), [], half, in_place(self.tokens), in_place(self.cotangent),
        )

    def add_terms(self, second):
        half = self.steps // 2
        _, others, _ = self.specs(half * second)
        last = self.depth // self.width
        cotangents = pl.BlockSpec((self.count, self.width), lambda i, where: (0, last))
        operands, in_specs = [self.terms[second]], [pl.BlockSpec((self.tile, self.width), lambda i, where: (i, 0))]
        for a, b in zip(self.first, self.second):
            operands += [in_place(value) for value in (a, b, a, b)]
            in_specs += others + [cotangents] * 2
        self.grad = self.call(
            grad_kernel, "grad", jax.ShapeDtypeStruct((self.depth, self.width), bf16), in_specs + [in_hbm] * second,
            pl.BlockSpec((self.tile, self.width), lambda i, where: (half * second + i, 0)), [], half,
            *operands, *([self.grad] if second else []), aliases={len(operands): 0} if second else {},
        )

    def wait_first(self, gate):
        gate, *self.first = after((gate, *self.first))
        return gate

    def early(self, j, gate, whole):
        self.chain.gates = [gate]
        term = self.own_term(len(self.terms))
        whole, term = after((whole, term))
        self.terms.append(term)
        return whole

    def finish_keys(self):
        def kernel(where_ref, keys_ref, *refs):
            total = keys_ref[...]
            for ref in refs[:-1]:
                total = total + ref[...].astype(f32)
            refs[-1][...] = total.astype(bf16)

        rows = pl.BlockSpec((self.count // 2, self.width), lambda i, where: (i, 0))
        self.keys = self.call(
            kernel, "finish_keys", self.result(bf16), [rows] * (2 + len(self.came)), rows, [], 2, self.keys, self.second_keys, *self.came
        )

    def late(self, k):
        if k == 1:
            self.keys = self.multiply_keys([in_place(self.tokens)], f32, 0)
        if k == 3:
            self.second_keys = self.multiply_keys([in_place(self.tokens)], f32, 1)
        if k == 2:
            others = [
                self.multiply_keys([in_place(value) for value in pair], bf16) for pair in zip(self.first, self.second)
            ]
            self.came = [self.shift(value, self.parts - s) for s, value in enumerate(others, 1)]
        if k in (4, 5):
            self.add_terms(k - 4)
        if k == 6:
            self.finish_keys()


def shards(tokens, inner_weight, cotangent, local_weights, anchor, momentum):
    chain = Chain()
    inner = Inner(chain, tokens, inner_weight, cotangent)
    new_weights, new_momentum = outer_step(chain, local_weights, anchor, momentum, inner)
    return (inner.keys, inner.grad[None], new_weights, new_momentum)


def solution(mesh):
    return jax.shard_map(
        shards,
        mesh=mesh,
        in_specs=(
            P(("replica", "fsdp"), None),
            P("replica", "fsdp", None),
            P(("replica", "fsdp"), None),
            P("replica", None, "fsdp", None),
            P(None, "fsdp", "replica", None),
            P(None, "fsdp", "replica", None),
        ),
        out_specs=(
            P(("replica", "fsdp"), None),
            P("replica", "fsdp", None),
            P(None, "fsdp", None),
            P(None, "fsdp", "replica", None),
        ),
        check_vma=False,
    )
```
